512 devices in a mesh: pb: 64 (over y, z), row: 4 (over x), col: 2 (over core).
Axes of the slice: x: 4, y: 8, z: 8, core: 2. Of those that a mesh axis runs over, the one named last changes fastest.
Arguments:
- amplitudes: bfloat16 [64, 20, 4, 9216], P('pb'), may hold values from -6 to 6
- pairs: int32 [64, 4, 2], P('pb'), may hold values from 0 to 63
- stored_k: int32 [64], replicated, may hold values from 0 to 63, each once
- orbitals: bfloat16 [64, 192, 2048], P('pb', None, ('row', 'col')), may hold values from -1.078125 to 1.078125
- valence_energy: float32 [64, 96], replicated, may hold values from -1 to 0
- conduction_energy: float32 [64, 96], replicated, may hold values from 2.5 to 3.5
- screened: bfloat16 [64, 2048, 2048], P('pb', 'row', 'col'), may hold values from -0.125 to 0.125
Outputs:
- filtered: bfloat16 [64, 20, 4, 9216], P('pb')
The draws below stay inside these ranges and needn't reach their ends.
Inputs may be any that keep to these rules, and one draw needn't show every extreme that they name: stored_k holds every k-point exactly once; row s of orbitals belongs to k-point stored_k[s]. `pairs`: each entry is a k-point.
All inputs are finite; a program needn't handle non-finite values.
Results may differ from the reference program's by a relative error of at most 0.024.
Values may be sent and summed in bfloat16 or wider, within the bound.
No kernel may reach another device: no remote copies, remote signals or barrier semaphores. Data moves between devices by JAX's collectives and lax.ppermute only.
A program may use at most 64 MiB of HBM per device.

```python
import jax
import jax.numpy as jnp
from jax import lax

NV = 96
NC = 96
NB = 192
NP = 2048
PAIRS = 4
NVEC = 20
NQ = 64
NK = 64
N_ROW = 4
N_COL = 2


def plant(values, stream_key, smallest, top_value):
    index_at = [jax.random.randint(jax.random.fold_in(stream_key, axis), (), 0, length) for axis, length in enumerate(values.shape)]
    widest = values.shape.index(max(values.shape))
    neighbour = index_at[:widest] + [(index_at[widest] + 1) % values.shape[widest]] + index_at[widest + 1:]
    return values.at[tuple(index_at)].set(smallest).at[tuple(neighbour)].set(top_value)


def block_levels(own_key, extent, split, least, top_value):
    factor_of, own = 1.0, jax.random.fold_in(own_key, 6)
    for position, blocks in split:
        steps = jnp.exp(jax.random.uniform(jax.random.fold_in(own, position), (blocks,), jnp.float32, least / len(split), top_value / len(split)))
        factor_of = factor_of * jnp.repeat(steps, extent[position] // blocks).reshape([-1 if axis == position else 1 for axis in range(len(extent))])
    return factor_of


def centred(key, shape, deviation, bound, cuts=(), kind=jnp.bfloat16):
    result = jax.random.normal(key, shape, jnp.float32) * deviation
    if len(cuts) > 0:
        result = block_levels(key, shape, cuts, -0.22, 0.18) * result
    return jnp.clip(result, min=-bound, max=bound).astype(kind)


def setup_inputs(seed: int = 0) -> dict:
    streams_of = jax.random.split(jax.random.key(seed), 8)
    amplitudes = centred(streams_of[0], (NQ, NVEC, PAIRS, NV * NC), 1.0, 6.0, ((0, 64),))
    pairs = plant(jax.random.randint(streams_of[1], (NQ, PAIRS, 2), 0, NK), jax.random.fold_in(streams_of[1], 1), 0, NK - 1).astype(jnp.int32)
    stored_k = jax.random.permutation(streams_of[2], NK).astype(jnp.int32)
    orbitals = centred(streams_of[3], (NK, NB, NP), 0.18, 1.078125, ((0, 64), (2, 8)))
    valence_energy = jnp.clip(jax.random.uniform(streams_of[4], (NK, NV), jnp.float32, -1.0, 0.0), -1.0, 0.0)
    conduction_energy = jnp.clip(jax.random.uniform(streams_of[5], (NK, NC), jnp.float32, 2.5, 3.5), 2.5, 3.5)
    screened = centred(streams_of[6], (NQ, NP, NP), NP ** -0.5, 0.125, ((0, 64), (1, 4), (2, 2)))
    return dict(amplitudes=amplitudes, pairs=pairs, stored_k=stored_k, orbitals=orbitals, valence_energy=valence_energy, conduction_energy=conduction_energy, screened=screened)


CENTER = 3.0
HALF = 2.5


def kernel_apply(amplitude, valence, conduction_orbital, w_matrix):
    block_count = N_ROW * N_COL
    block_width = NP // block_count
    amplitude_lattice = amplitude.reshape(NVEC, PAIRS, NV, NC).astype(jnp.float32)
    inner_total_sum = jnp.einsum("iomx,oxj->iomj", amplitude_lattice, conduction_orbital.astype(jnp.float32))
    values = jnp.sum(valence.astype(jnp.float32)[None] * inner_total_sum, axis=2)
    values = values.astype(jnp.bfloat16).reshape(NVEC * PAIRS, NP)
    screened_values = jnp.dot(values, w_matrix.T, preferred_element_type=jnp.float32)
    screened_values = screened_values.reshape(NVEC, PAIRS, NP)
    weighted_product = (valence.astype(jnp.float32)[None] * screened_values[:, :, None, :]).astype(jnp.bfloat16)

    def block_sum(running, block_id):
        screened_portion = lax.dynamic_slice_in_dim(weighted_product, block_id * block_width, block_width, 3)
        conduction_portion = lax.dynamic_slice_in_dim(conduction_orbital, block_id * block_width, block_width, 2)
        block_contribution = jnp.einsum("kyqz,yhz->kyqh", screened_portion.astype(jnp.float32), conduction_portion.astype(jnp.float32))
        rounded = lax.optimization_barrier(block_contribution.astype(jnp.bfloat16))
        return running + rounded.astype(jnp.float32), None

    zeros_init = jnp.zeros((NVEC, PAIRS, NV, NC), jnp.float32)
    running, _ = lax.scan(block_sum, zeros_init, jnp.arange(block_count, dtype=jnp.int32))
    return running.reshape(NVEC, PAIRS, NV * NC)


def scaled(current, kernel_term, gap_grid):
    return (gap_grid[None] * current + kernel_term - CENTER * current) / HALF


def reference(amplitudes, pairs, stored_k, orbitals, valence_energy, conduction_energy, screened):
    inverse = jnp.zeros((NK,), jnp.int32).at[stored_k].set(jnp.arange(NK, dtype=jnp.int32))

    def per_transfer(inputs):
        amplitude, pair_list, w_matrix = inputs
        valence = orbitals[inverse[pair_list[:, 0]], :NV]
        conduction_orbital = orbitals[inverse[pair_list[:, 1]], NV:]
        low_energy = jnp.take(valence_energy, pair_list[:, 0], axis=0)
        high_energy = jnp.take(conduction_energy, pair_list[:, 1], axis=0)
        gap_grid = (high_energy[:, None, :] - low_energy[:, :, None]).reshape(PAIRS, NV * NC)
        initial = amplitude.astype(jnp.float32)
        first_term = scaled(initial, kernel_apply(amplitude, valence, conduction_orbital, w_matrix), gap_grid).astype(jnp.bfloat16)
        second_term = scaled(first_term.astype(jnp.float32), kernel_apply(first_term, valence, conduction_orbital, w_matrix), gap_grid)
        return (2.0 * second_term - initial).astype(jnp.bfloat16)

    return lax.map(per_transfer, (amplitudes, pairs, screened))
```

```python
import jax
import jax.numpy as jnp
from jax import lax
from jax.experimental import pallas as pl
from jax.experimental.pallas import tpu as pltpu
from jax.sharding import PartitionSpec as P

CENTER = 3.0
HALF = 2.5
LANES = 128
ROWS = 8
VMEM_LIMIT = 56 * 1024 * 1024


def pack_kernel(pairs_ref, stored_ref, orbitals_ref, out_ref):
    targets = out_ref.shape[0]
    count = pairs_ref.shape[1]
    stored = stored_ref[...]
    place = lax.broadcasted_iota(jnp.int32, stored.shape, 1).astype(jnp.float32)
    lane = lax.broadcasted_iota(jnp.int32, (ROWS, LANES), 1)
    wanted = jnp.zeros((ROWS, LANES), jnp.float32)
    for half in range(2):
        for pair in range(count):
            hit = stored == pairs_ref[0, pair, half]
            row = jnp.sum(jnp.where(hit, place, 0.0), axis=1, keepdims=True)
            wanted = jnp.where(lane == half * count + pair, row, wanted)
    bands = orbitals_ref.shape[1]
    wide = orbitals_ref.shape[2] // LANES
    tiles = bands // ROWS * wide
    for target in range(targets):
        if target < tiles:
            group, side = target // wide, target % wide
            tile = orbitals_ref[0, group * ROWS : (group + 1) * ROWS, side * LANES : (side + 1) * LANES]
            tile = tile.astype(jnp.float32)
        else:
            tile = jnp.zeros((ROWS, LANES), jnp.float32)
        out_ref[target] = jnp.concatenate([tile, wanted], axis=0).astype(jnp.bfloat16)


def select_kernel(rows_ref, table_ref, out_ref):
    transfers, count = rows_ref.shape

    def one(transfer, carry):
        for pair in range(count):
            out_ref[transfer * count + pair] = table_ref[rows_ref[transfer, pair], :ROWS, :]
        return carry

    lax.fori_loop(0, transfers, one, 0, unroll=8)


def steps_kernel(column_ref, gap_ref, own_ref, other_ref, start_ref, w_ref, out_ref,
                 valence, conduction, w_all, screened_in, screened_out, total, first, sems):
    count_v = valence.shape[0]
    count_c = conduction.shape[0]
    points = valence.shape[1]
    tiles_w = w_ref.shape[0]
    rows_w, cols_w = w_ref.shape[1], w_ref.shape[2]
    wide_w = points // cols_w
    flat_rows = start_ref.shape[0]
    vectors = flat_rows // count_v
    padded = screened_in.shape[0]
    copies = [pltpu.make_async_copy(w_ref.at[t], w_all.at[t], sems.at[t]) for t in range(tiles_w)]
    for copy in copies:
        copy.start()

    even = column_ref[0] == 0
    wide = 2
    row_count = points // (2 * wide * LANES)

    def fetch(tile, block):
        row, core = block // 2, block % 2
        mine = own_ref[tile * row_count + row].astype(jnp.float32)
        theirs = other_ref[tile * row_count + row].astype(jnp.float32)
        return jnp.where(even, mine, theirs) if core == 0 else jnp.where(even, theirs, mine)

    for block in range(2 * row_count):
        for side in range(wide):
            lanes = slice((block * wide + side) * LANES, (block * wide + side + 1) * LANES)
            for pack in range(count_v // (2 * ROWS)):
                tile = [fetch((2 * pack + k) * wide + side, block) for k in range(2)]
                valence[2 * pack * ROWS : 2 * (pack + 1) * ROWS, lanes] = jnp.concatenate(tile, axis=0)
            base = count_v // ROWS
            for pack in range(count_c // (2 * ROWS)):
                tile = [fetch((base + 2 * pack + k) * wide + side, block) for k in range(2)]
                conduction[2 * pack * ROWS : 2 * (pack + 1) * ROWS, lanes] = jnp.concatenate(
                    tile, axis=0
                ).astype(jnp.bfloat16)

    screened_in[...] = jnp.zeros_like(screened_in)
    chunk = 256
    chunks = points // chunk

    def kernel_term(current_ref):
        def expand(step, carry):
            lanes = pl.ds(pl.multiple_of(step * chunk, chunk), chunk)
            inner = jnp.dot(current_ref[...], conduction[:, lanes], preferred_element_type=jnp.float32)
            inner = inner.reshape(vectors, count_v, chunk) * valence[:, lanes][None]
            screened_in[:vectors, lanes] = jnp.sum(inner, axis=1).astype(jnp.bfloat16).astype(jnp.float32)
            return carry

        lax.fori_loop(0, chunks, expand, 0)
        values = screened_in[...].astype(jnp.bfloat16)
        if current_ref is start_ref:
            for copy in copies:
                copy.wait()
        for row in range(tiles_w // wide_w):
            summed = jnp.zeros((padded, rows_w), jnp.float32)
            for col in range(wide_w):
                summed += lax.dot_general(
                    values[:, col * cols_w : (col + 1) * cols_w],
                    w_all[row * wide_w + col],
                    (((1,), (1,)), ((), ())),
                    preferred_element_type=jnp.float32,
                )
            screened_out[:, row * rows_w : (row + 1) * rows_w] = summed
        total[...] = jnp.zeros_like(total)

        def project(step, carry):
            lanes = pl.ds(pl.multiple_of(step * chunk, chunk), chunk)
            weighted = screened_out[:vectors, lanes][:, None, :] * valence[:, lanes][None]
            weighted = weighted.reshape(flat_rows, chunk).astype(jnp.bfloat16)
            total[...] += lax.dot_general(
                weighted,
                conduction[:, lanes],
                (((1,), (1,)), ((), ())),
                preferred_element_type=jnp.float32,
            )
            return carry

        lax.fori_loop(0, chunks, project, 0)

    gap = gap_ref[...][None]

    def scaled(current):
        parts = current.astype(jnp.float32).reshape(vectors, count_v, count_c)
        term = total[...].reshape(vectors, count_v, count_c)
        return ((gap * parts + term - CENTER * parts) / HALF).reshape(flat_rows, count_c)

    kernel_term(start_ref)
    first[...] = scaled(start_ref[...]).astype(jnp.bfloat16)
    kernel_term(first)
    out_ref[...] = (2.0 * scaled(first[...]) - start_ref[...].astype(jnp.float32)).astype(jnp.bfloat16)


def on_device(amplitudes, pairs, stored_k, orbitals, valence_energy, conduction_energy, screened):
    transfers = stored_k.shape[0]
    count_v = valence_energy.shape[1]
    count_c = conduction_energy.shape[1]
    vectors, pair_count, flat_size = amplitudes.shape[1:]
    member = lax.axis_index("pb")
    pair = lax.axis_index("row")
    column = lax.axis_index("col")
    cols = lax.axis_size("col")
    devices = lax.axis_size("row") * cols
    points = orbitals.shape[2] * devices
    share = vectors // cols
    smem = pl.BlockSpec(memory_space=pltpu.SMEM)
    vmem = pl.BlockSpec(memory_space=pltpu.VMEM)
    limit = pltpu.CompilerParams(vmem_limit_bytes=VMEM_LIMIT)

    w_tiles = lax.all_gather(screened[0], ("row", "col"))

    message = pl.pallas_call(
        pack_kernel,
        out_shape=jax.ShapeDtypeStruct((transfers, 2 * ROWS, LANES), jnp.bfloat16),
        in_specs=[smem, vmem, vmem],
        out_specs=vmem,
        compiler_params=limit,
    )(pairs, stored_k.reshape(1, transfers), orbitals)
    table = lax.all_to_all(message, "pb", 0, 0, tiled=True)
    wanted = table[:, ROWS, : 2 * pair_count].astype(jnp.int32)
    valence_tiles = count_v // ROWS * (orbitals.shape[2] // LANES)
    rows = jnp.where(member < valence_tiles, wanted[:, :pair_count], wanted[:, pair_count:])
    chosen = pl.pallas_call(
        select_kernel,
        out_shape=jax.ShapeDtypeStruct((transfers * pair_count, ROWS, LANES), jnp.bfloat16),
        in_specs=[smem, vmem],
        out_specs=vmem,
        compiler_params=limit,
    )(rows, table)
    own = lax.all_to_all(chosen, ("pb", "row"), 0, 0, tiled=True)
    other = lax.ppermute(own, "col", [(0, 1), (1, 0)])

    start = lax.dynamic_slice(
        amplitudes[0], (column * share, pair, 0), (share, 1, flat_size)
    ).reshape(share * count_v, count_c)
    listed = lax.dynamic_slice_in_dim(pairs[0], pair, 1, 0)
    low = lax.dynamic_slice_in_dim(valence_energy, listed[0, 0], 1, 0)
    high = lax.dynamic_slice_in_dim(conduction_energy, listed[0, 1], 1, 0)
    gap = high - low.reshape(count_v, 1)

    padded = 16
    flat_rows = share * count_v
    result = pl.pallas_call(
        steps_kernel,
        out_shape=jax.ShapeDtypeStruct((flat_rows, count_c), jnp.bfloat16),
        in_specs=[smem, vmem, vmem, vmem, vmem, pl.BlockSpec(memory_space=pl.ANY)],
        out_specs=vmem,
        scratch_shapes=[
            pltpu.VMEM((count_v, points), jnp.float32),
            pltpu.VMEM((count_c, points), jnp.bfloat16),
            pltpu.VMEM(w_tiles.shape, jnp.bfloat16),
            pltpu.VMEM((padded, points), jnp.float32),
            pltpu.VMEM((padded, points), jnp.float32),
            pltpu.VMEM((flat_rows, count_c), jnp.float32),
            pltpu.VMEM((flat_rows, count_c), jnp.bfloat16),
            pltpu.SemaphoreType.DMA((devices,)),
        ],
        compiler_params=limit,
    )(column.reshape(1), gap, own, other, start, w_tiles)

    mine = result.reshape(share, flat_size // LANES, LANES)
    across = lax.all_gather(mine, "row")
    theirs = lax.ppermute(across, "col", [(0, 1), (1, 0)])
    both = jnp.where(
        column == 0, jnp.stack([across, theirs]), jnp.stack([theirs, across])
    )
    return both.transpose(0, 2, 1, 3, 4).reshape(1, vectors, pair_count, flat_size)


def solution(mesh):
    return jax.shard_map(
        on_device,
        mesh=mesh,
        in_specs=(
            P("pb", None, None, None),
            P("pb", None, None),
            P(),
            P("pb", None, ("row", "col")),
            P(),
            P(),
            P("pb", "row", "col"),
        ),
        out_specs=P("pb", None, None, None),
        check_vma=False,
    )
```

```python
import jax
import jax.numpy as jnp
from jax import lax
from jax.experimental import pallas as pl
from jax.experimental.pallas import tpu as pltpu
from jax.sharding import PartitionSpec as P

CENTER = 3.0
HALF = 2.5
LANES = 128
ROWS = 8
VMEM_LIMIT = 56 * 1024 * 1024


def pack_kernel(pairs_ref, stored_ref, orbitals_ref, out_ref):
    targets = out_ref.shape[0]
    count = pairs_ref.shape[1]
    stored = stored_ref[...]
    place = lax.broadcasted_iota(jnp.int32, stored.shape, 1).astype(jnp.float32)
    lane = lax.broadcasted_iota(jnp.int32, (ROWS, LANES), 1)
    wanted = jnp.zeros((ROWS, LANES), jnp.float32)
    for half in range(2):
        for pair in range(count):
            hit = stored == pairs_ref[half, pair]
            row = jnp.sum(jnp.where(hit, place, 0.0), axis=1, keepdims=True)
            wanted = jnp.where(lane == half * count + pair, row, wanted)
    bands = orbitals_ref.shape[1]
    wide = orbitals_ref.shape[2] // LANES
    tiles = bands // ROWS * wide
    for target in range(targets):
        if target < tiles:
            group, side = target // wide, target % wide
            tile = orbitals_ref[0, group * ROWS : (group + 1) * ROWS, side * LANES : (side + 1) * LANES]
            tile = tile.astype(jnp.float32)
        else:
            tile = jnp.zeros((ROWS, LANES), jnp.float32)
        out_ref[target] = jnp.concatenate([tile, wanted], axis=0).astype(jnp.bfloat16)


def select_kernel(rows_ref, table_ref, out_ref):
    transfers, count = rows_ref.shape

    def one(transfer, carry):
        for pair in range(count):
            out_ref[transfer * count + pair] = table_ref[rows_ref[transfer, pair], :ROWS, :]
        return carry

    lax.fori_loop(0, transfers, one, 0, unroll=8)


def steps_kernel(place_ref, gap_ref, own_ref, other_ref, start_ref, *refs):
    tiles_w = len(refs) - 10
    w_refs, out_ref = refs[:tiles_w], refs[tiles_w]
    valence, conduction, w_all, screened_in, screened_out, total, first, flat, sems = refs[tiles_w + 1 :]
    count_v = valence.shape[0]
    count_c = conduction.shape[0]
    points = valence.shape[1]
    rows_w, cols_w = w_refs[0].shape
    wide_w = points // cols_w
    flat_rows = start_ref.shape[0]
    vectors = flat_rows // count_v
    padded = screened_in.shape[0]
    copies = [
        pltpu.make_async_copy(w_refs[t], w_all.at[place_ref[1 + t]], sems.at[t]) for t in range(tiles_w)
    ]
    for copy in copies:
        copy.start()

    even = place_ref[0] == 0
    wide = 2
    row_count = points // (2 * wide * LANES)

    def fetch(tile, block):
        row, core = block // 2, block % 2
        mine = own_ref[tile * row_count + row].astype(jnp.float32)
        theirs = other_ref[tile * row_count + row].astype(jnp.float32)
        return jnp.where(even, mine, theirs) if core == 0 else jnp.where(even, theirs, mine)

    for block in range(2 * row_count):
        for side in range(wide):
            lanes = slice((block * wide + side) * LANES, (block * wide + side + 1) * LANES)
            for pack in range(count_v // (2 * ROWS)):
                tile = [fetch((2 * pack + k) * wide + side, block) for k in range(2)]
                valence[2 * pack * ROWS : 2 * (pack + 1) * ROWS, lanes] = jnp.concatenate(tile, axis=0)
            base = count_v // ROWS
            for pack in range(count_c // (2 * ROWS)):
                tile = [fetch((base + 2 * pack + k) * wide + side, block) for k in range(2)]
                conduction[2 * pack * ROWS : 2 * (pack + 1) * ROWS, lanes] = jnp.concatenate(
                    tile, axis=0
                ).astype(jnp.bfloat16)

    screened_in[...] = jnp.zeros_like(screened_in)
    chunk = 256
    chunks = points // chunk

    def kernel_term(current_ref):
        def expand(step, carry):
            lanes = pl.ds(pl.multiple_of(step * chunk, chunk), chunk)
            inner = jnp.dot(current_ref[...], conduction[:, lanes], preferred_element_type=jnp.float32)
            inner = inner.reshape(vectors, count_v, chunk) * valence[:, lanes][None]
            screened_in[:vectors, lanes] = jnp.sum(inner, axis=1).astype(jnp.bfloat16).astype(jnp.float32)
            return carry

        lax.fori_loop(0, chunks, expand, 0)
        values = screened_in[...].astype(jnp.bfloat16)
        if current_ref is start_ref:
            for copy in copies:
                copy.wait()
        for row in range(tiles_w // wide_w):
            summed = jnp.zeros((padded, rows_w), jnp.float32)
            for col in range(wide_w):
                summed += lax.dot_general(
                    values[:, col * cols_w : (col + 1) * cols_w],
                    w_all[row * wide_w + col],
                    (((1,), (1,)), ((), ())),
                    preferred_element_type=jnp.float32,
                )
            screened_out[:, row * rows_w : (row + 1) * rows_w] = summed
        total[...] = jnp.zeros_like(total)

        def project(step, carry):
            lanes = pl.ds(pl.multiple_of(step * chunk, chunk), chunk)
            weighted = screened_out[:vectors, lanes][:, None, :] * valence[:, lanes][None]
            weighted = weighted.reshape(flat_rows, chunk).astype(jnp.bfloat16)
            total[...] += lax.dot_general(
                weighted,
                conduction[:, lanes],
                (((1,), (1,)), ((), ())),
                preferred_element_type=jnp.float32,
            )
            return carry

        lax.fori_loop(0, chunks, project, 0)

    gap = gap_ref[...][None]

    def scaled(current):
        parts = current.astype(jnp.float32).reshape(vectors, count_v, count_c)
        term = total[...].reshape(vectors, count_v, count_c)
        return ((gap * parts + term - CENTER * parts) / HALF).reshape(flat_rows, count_c)

    kernel_term(start_ref)
    first[...] = scaled(start_ref[...]).astype(jnp.bfloat16)
    kernel_term(first)
    total[...] = 2.0 * scaled(first[...]) - start_ref[...].astype(jnp.float32)

    quads = flat_rows // 4
    part = [total[pl.ds(k, quads, stride=4), :] for k in range(4)]
    third = LANES - count_c
    flat[pl.ds(0, quads, stride=3), :] = jnp.concatenate([part[0], part[1][:, :third]], axis=1)
    flat[pl.ds(1, quads, stride=3), :] = jnp.concatenate([part[1][:, third:], part[2][:, : 2 * third]], axis=1)
    flat[pl.ds(2, quads, stride=3), :] = jnp.concatenate([part[2][:, 2 * third :], part[3]], axis=1)
    out_ref[...] = flat[...].astype(jnp.bfloat16)


def on_device(amplitudes, pairs, stored_k, orbitals, valence_energy, conduction_energy, screened):
    transfers = stored_k.shape[0]
    count_v = valence_energy.shape[1]
    count_c = conduction_energy.shape[1]
    vectors, pair_count, flat_size = amplitudes.shape[1:]
    member = lax.axis_index("pb")
    pair = lax.axis_index("row")
    column = lax.axis_index("col")
    cols = lax.axis_size("col")
    devices = lax.axis_size("row") * cols
    points = orbitals.shape[2] * devices
    share = vectors // cols
    smem = pl.BlockSpec(memory_space=pltpu.SMEM)
    vmem = pl.BlockSpec(memory_space=pltpu.VMEM)
    limit = pltpu.CompilerParams(vmem_limit_bytes=VMEM_LIMIT)

    message = pl.pallas_call(
        pack_kernel,
        out_shape=jax.ShapeDtypeStruct((transfers, 2 * ROWS, LANES), jnp.bfloat16),
        in_specs=[smem, vmem, vmem],
        out_specs=vmem,
        compiler_params=limit,
    )(pairs[0].T, stored_k.reshape(1, transfers), orbitals)
    table = lax.all_to_all(message, "pb", 0, 0, tiled=True)

    swap = [(0, 1), (1, 0)]
    rows_axis = lax.axis_size("row")
    ring = [(r, c) for r in range(rows_axis) for c in range(cols)]
    there = [(r * cols + c, (r + 1 - 2 * c) % rows_axis * cols + c) for r, c in ring]
    back = [(target, source) for source, target in there]
    w_own, _ = lax.optimization_barrier((screened[0], message))
    w_there = lax.ppermute(w_own, ("row", "col"), there)
    w_back = lax.ppermute(w_own, ("row", "col"), back)
    w_far = lax.ppermute(w_there, ("row", "col"), there)
    w_mine = [w_own, w_there, w_back, w_far]
    w_tiles = w_mine + [lax.ppermute(tile, "col", swap) for tile in w_mine]
    turn = 1 - 2 * column
    rows_mine = jnp.stack([pair, pair - turn, pair + turn, pair + 2]) % rows_axis
    rows_theirs = jnp.stack([pair, pair + turn, pair - turn, pair + 2]) % rows_axis
    place = jnp.concatenate(
        [column.reshape(1), rows_mine * cols + column, rows_theirs * cols + 1 - column]
    ).astype(jnp.int32)
    start = lax.dynamic_slice(
        amplitudes[0], (column * share, pair, 0), (share, 1, flat_size)
    ).reshape(share * count_v, count_c)
    listed = lax.dynamic_slice_in_dim(pairs[0], pair, 1, 0)
    low = lax.dynamic_slice_in_dim(valence_energy, listed[0, 0], 1, 0)
    high = lax.dynamic_slice_in_dim(conduction_energy, listed[0, 1], 1, 0)
    gap = high - low.reshape(count_v, 1)

    table, start, gap, place = lax.optimization_barrier((table, start, gap, place))

    wanted = table[:, ROWS, : 2 * pair_count].astype(jnp.int32)
    valence_tiles = count_v // ROWS * (orbitals.shape[2] // LANES)
    rows = jnp.where(member < valence_tiles, wanted[:, :pair_count], wanted[:, pair_count:])
    chosen = pl.pallas_call(
        select_kernel,
        out_shape=jax.ShapeDtypeStruct((transfers * pair_count, ROWS, LANES), jnp.bfloat16),
        in_specs=[smem, vmem],
        out_specs=vmem,
        compiler_params=limit,
    )(rows, table)
    own = lax.all_to_all(chosen, ("pb", "row"), 0, 0, tiled=True)
    other = lax.ppermute(own, "col", [(0, 1), (1, 0)])

    padded = 16
    flat_rows = share * count_v
    result = pl.pallas_call(
        steps_kernel,
        out_shape=jax.ShapeDtypeStruct((flat_rows * count_c // LANES, LANES), jnp.bfloat16),
        in_specs=[smem, vmem, vmem, vmem, vmem] + [pl.BlockSpec(memory_space=pl.ANY)] * devices,
        out_specs=vmem,
        scratch_shapes=[
            pltpu.VMEM((count_v, points), jnp.float32),
            pltpu.VMEM((count_c, points), jnp.bfloat16),
            pltpu.VMEM((devices,) + screened.shape[1:], jnp.bfloat16),
            pltpu.VMEM((padded, points), jnp.float32),
            pltpu.VMEM((padded, points), jnp.float32),
            pltpu.VMEM((flat_rows, count_c), jnp.float32),
            pltpu.VMEM((flat_rows, count_c), jnp.bfloat16),
            pltpu.VMEM((flat_rows * count_c // LANES, LANES), jnp.float32),
            pltpu.SemaphoreType.DMA((devices,)),
        ],
        compiler_params=limit,
    )(place, gap, own, other, start, *w_tiles)

    mine = result.reshape(share, flat_size // LANES, LANES)
    across = lax.all_gather(mine, "row")
    theirs = lax.ppermute(across, "col", [(0, 1), (1, 0)])
    both = jnp.where(
        column == 0, jnp.stack([across, theirs]), jnp.stack([theirs, across])
    )
    return both.transpose(0, 2, 1, 3, 4).reshape(1, vectors, pair_count, flat_size)


def solution(mesh):
    return jax.shard_map(
        on_device,
        mesh=mesh,
        in_specs=(
            P("pb", None, None, None),
            P("pb", None, None),
            P(),
            P("pb", None, ("row", "col")),
            P(),
            P(),
            P("pb", "row", "col"),
        ),
        out_specs=P("pb", None, None, None),
        check_vma=False,
    )
```

```python
import jax
import jax.numpy as jnp
from jax import lax
from jax.experimental import pallas as pl
from jax.experimental.pallas import tpu as pltpu
from jax.sharding import PartitionSpec as P

CENTER = 3.0
HALF = 2.5
LANES = 128
ROWS = 8
VMEM_LIMIT = 56 * 1024 * 1024


def pack_kernel(pairs_ref, stored_ref, orbitals_ref, out_ref):
    targets = out_ref.shape[0]
    count = pairs_ref.shape[1]
    stored = stored_ref[...]
    place = lax.broadcasted_iota(jnp.int32, stored.shape, 1).astype(jnp.float32)
    lane = lax.broadcasted_iota(jnp.int32, (ROWS, LANES), 1)
    wanted = jnp.zeros((ROWS, LANES), jnp.float32)
    for half in range(2):
        for pair in range(count):
            hit = stored == pairs_ref[half, pair]
            row = jnp.sum(jnp.where(hit, place, 0.0), axis=1, keepdims=True)
            wanted = jnp.where(lane == half * count + pair, row, wanted)
    bands = orbitals_ref.shape[1]
    wide = orbitals_ref.shape[2] // LANES
    tiles = bands // ROWS * wide
    for target in range(targets):
        if target < tiles:
            group, side = target // wide, target % wide
            tile = orbitals_ref[0, group * ROWS : (group + 1) * ROWS, side * LANES : (side + 1) * LANES]
            tile = tile.astype(jnp.float32)
        else:
            tile = jnp.zeros((ROWS, LANES), jnp.float32)
        out_ref[target] = jnp.concatenate([tile, wanted], axis=0).astype(jnp.bfloat16)


def select_kernel(rows_ref, table_ref, out_ref):
    transfers, count = rows_ref.shape

    def one(transfer, carry):
        for pair in range(count):
            out_ref[transfer * count + pair] = table_ref[rows_ref[transfer, pair], :ROWS, :]
        return carry

    lax.fori_loop(0, transfers, one, 0, unroll=8)


def steps_kernel(pairs_ref, low_ref, high_ref, own_ref, other_ref, start_ref, *refs):
    tiles_w = len(refs) - 10
    pair, column = lax.axis_index("row"), lax.axis_index("col")
    w_refs, out_ref = refs[:tiles_w], refs[tiles_w]
    valence, conduction, w_all, screened_in, screened_out, total, first, flat, sems = refs[tiles_w + 1 :]
    count_v = valence.shape[0]
    count_c = conduction.shape[0]
    points = valence.shape[1]
    rows_w, cols_w = w_refs[0].shape
    wide_w = points // cols_w
    flat_rows = start_ref.shape[0]
    vectors = flat_rows // count_v
    padded = screened_in.shape[0]
    turn = 1 - 2 * column
    steps = (0, -turn, turn, 2, 0, turn, -turn, 2)
    sides = (column,) * 4 + (1 - column,) * 4
    copies = [
        pltpu.make_async_copy(w_refs[t], w_all.at[(pair + steps[t] + 4) % 4 * 2 + sides[t]], sems.at[t])
        for t in range(tiles_w)
    ]
    for copy in copies:
        copy.start()

    even = column == 0
    wide = 2
    row_count = points // (2 * wide * LANES)

    def fetch(tile, block):
        row, core = block // 2, block % 2
        mine = own_ref[tile * row_count + row].astype(jnp.float32)
        theirs = other_ref[tile * row_count + row].astype(jnp.float32)
        return jnp.where(even, mine, theirs) if core == 0 else jnp.where(even, theirs, mine)

    for block in range(2 * row_count):
        for side in range(wide):
            lanes = slice((block * wide + side) * LANES, (block * wide + side + 1) * LANES)
            for pack in range(count_v // (2 * ROWS)):
                tile = [fetch((2 * pack + k) * wide + side, block) for k in range(2)]
                valence[2 * pack * ROWS : 2 * (pack + 1) * ROWS, lanes] = jnp.concatenate(tile, axis=0)
            base = count_v // ROWS
            for pack in range(count_c // (2 * ROWS)):
                tile = [fetch((base + 2 * pack + k) * wide + side, block) for k in range(2)]
                conduction[2 * pack * ROWS : 2 * (pack + 1) * ROWS, lanes] = jnp.concatenate(
                    tile, axis=0
                ).astype(jnp.bfloat16)

    screened_in[...] = jnp.zeros_like(screened_in)

    def kernel_term(current_ref):
        inner = jnp.dot(current_ref[...], conduction[...], preferred_element_type=jnp.float32)
        inner = inner.reshape(vectors, count_v, points) * valence[...][None]
        screened_in[:vectors, :] = jnp.sum(inner, axis=1)
        values = screened_in[...].astype(jnp.bfloat16)
        if current_ref is start_ref:
            for copy in copies:
                copy.wait()
        for row in range(tiles_w // wide_w):
            summed = jnp.zeros((padded, rows_w), jnp.float32)
            for col in range(wide_w):
                summed += lax.dot_general(
                    values[:, col * cols_w : (col + 1) * cols_w],
                    w_all[row * wide_w + col],
                    (((1,), (1,)), ((), ())),
                    preferred_element_type=jnp.float32,
                )
            screened_out[:, row * rows_w : (row + 1) * rows_w] = summed
        weighted = screened_out[:vectors, :][:, None, :] * valence[...][None]
        weighted = weighted.reshape(flat_rows, points).astype(jnp.bfloat16)
        total[...] = lax.dot_general(
            weighted, conduction[...], (((1,), (1,)), ((), ())), preferred_element_type=jnp.float32
        )

    low = low_ref[pl.ds(pairs_ref[0, pair], 1), :]
    high = high_ref[pl.ds(pairs_ref[1, pair], 1), :]
    square = (count_v, count_v)
    diagonal = lax.broadcasted_iota(jnp.int32, square, 0) == lax.broadcasted_iota(jnp.int32, square, 1)
    low = jnp.sum(jnp.where(diagonal, low, 0.0), axis=1, keepdims=True)
    gap = (high - low)[None]

    def scaled(current):
        parts = current.astype(jnp.float32).reshape(vectors, count_v, count_c)
        term = total[...].reshape(vectors, count_v, count_c)
        return ((gap * parts + term - CENTER * parts) / HALF).reshape(flat_rows, count_c)

    kernel_term(start_ref)
    first[...] = scaled(start_ref[...]).astype(jnp.bfloat16)
    kernel_term(first)
    total[...] = 2.0 * scaled(first[...]) - start_ref[...].astype(jnp.float32)

    quads = flat_rows // 4
    part = [total[pl.ds(k, quads, stride=4), :] for k in range(4)]
    third = LANES - count_c
    flat[pl.ds(0, quads, stride=3), :] = jnp.concatenate([part[0], part[1][:, :third]], axis=1)
    flat[pl.ds(1, quads, stride=3), :] = jnp.concatenate([part[1][:, third:], part[2][:, : 2 * third]], axis=1)
    flat[pl.ds(2, quads, stride=3), :] = jnp.concatenate([part[2][:, 2 * third :], part[3]], axis=1)
    out_ref[...] = flat[...].astype(jnp.bfloat16)


def on_device(amplitudes, pairs, stored_k, orbitals, valence_energy, conduction_energy, screened):
    transfers = stored_k.shape[0]
    count_v = valence_energy.shape[1]
    count_c = conduction_energy.shape[1]
    vectors, pair_count, flat_size = amplitudes.shape[1:]
    member = lax.axis_index("pb")
    pair = lax.axis_index("row")
    column = lax.axis_index("col")
    rows_axis, cols = lax.axis_size("row"), lax.axis_size("col")
    devices = rows_axis * cols
    points = orbitals.shape[2] * devices
    share = vectors // cols
    flat_rows = share * count_v
    padded = 16
    smem = pl.BlockSpec(memory_space=pltpu.SMEM)
    vmem = pl.BlockSpec(memory_space=pltpu.VMEM)
    anywhere = pl.BlockSpec(memory_space=pl.ANY)
    limit = pltpu.CompilerParams(vmem_limit_bytes=VMEM_LIMIT)
    swap = [(0, 1), (1, 0)]
    ring = [(r, c) for r in range(rows_axis) for c in range(cols)]
    there = [(r * cols + c, (r + 1 - 2 * c) % rows_axis * cols + c) for r, c in ring]
    back = [(target, source) for source, target in there]

    wishes = pairs[0].T
    message = pl.pallas_call(
        pack_kernel,
        out_shape=jax.ShapeDtypeStruct((transfers, 2 * ROWS, LANES), jnp.bfloat16),
        in_specs=[smem, vmem, vmem],
        out_specs=vmem,
        compiler_params=limit,
    )(wishes, stored_k.reshape(1, transfers), orbitals)
    table = lax.all_to_all(message, "pb", 0, 0, tiled=True)

    start = lax.dynamic_slice(
        amplitudes[0],
        (column * share, pair, 0),
        (share, 1, flat_size),
        allow_negative_indices=False,
    ).reshape(flat_rows, count_c)
    w_own, _ = lax.optimization_barrier((screened[0], message))
    w_there = lax.ppermute(w_own, ("row", "col"), there)
    w_back = lax.ppermute(w_own, ("row", "col"), back)

    w_far = lax.ppermute(w_there, ("row", "col"), there)
    table, start = lax.optimization_barrier((table, start))

    wanted = table[:, ROWS, : 2 * pair_count].astype(jnp.int32)
    valence_tiles = count_v // ROWS * (orbitals.shape[2] // LANES)
    rows = jnp.where(member < valence_tiles, wanted[:, :pair_count], wanted[:, pair_count:])
    chosen = pl.pallas_call(
        select_kernel,
        out_shape=jax.ShapeDtypeStruct((transfers * pair_count, ROWS, LANES), jnp.bfloat16),
        in_specs=[smem, vmem],
        out_specs=vmem,
        compiler_params=limit,
    )(rows, table)
    own = lax.all_to_all(chosen, ("pb", "row"), 0, 0, tiled=True)

    w_core = [w_own, w_there, w_back, w_far]
    w_tiles = w_core + [lax.ppermute(tile, "col", swap) for tile in w_core]
    other = lax.ppermute(own, "col", swap)

    result = pl.pallas_call(
        steps_kernel,
        out_shape=jax.ShapeDtypeStruct((flat_rows * count_c // LANES, LANES), jnp.bfloat16),
        in_specs=[smem, vmem, vmem, vmem, vmem, vmem] + [anywhere] * devices,
        out_specs=vmem,
        scratch_shapes=[
            pltpu.VMEM((count_v, points), jnp.float32),
            pltpu.VMEM((count_c, points), jnp.bfloat16),
            pltpu.VMEM((devices,) + screened.shape[1:], jnp.bfloat16),
            pltpu.VMEM((padded, points), jnp.float32),
            pltpu.VMEM((padded, points), jnp.float32),
            pltpu.VMEM((flat_rows, count_c), jnp.float32),
            pltpu.VMEM((flat_rows, count_c), jnp.bfloat16),
            pltpu.VMEM((flat_rows * count_c // LANES, LANES), jnp.float32),
            pltpu.SemaphoreType.DMA((devices,)),
        ],
        compiler_params=limit,
    )(wishes, valence_energy, conduction_energy, own, other, start, *w_tiles)

    mine = result.reshape(share, flat_size // LANES, LANES)
    across = lax.all_gather(mine, "row")
    theirs = lax.ppermute(across, "col", swap)
    both = jnp.where(column == 0, jnp.stack([across, theirs]), jnp.stack([theirs, across]))
    return both.transpose(0, 2, 1, 3, 4).reshape(1, vectors, pair_count, flat_size)


def solution(mesh):
    return jax.shard_map(
        on_device,
        mesh=mesh,
        in_specs=(
            P("pb", None, None, None),
            P("pb", None, None),
            P(),
            P("pb", None, ("row", "col")),
            P(),
            P(),
            P("pb", "row", "col"),
        ),
        out_specs=P("pb", None, None, None),
        check_vma=False,
    )
```

```python
import jax
import jax.numpy as jnp
from jax import lax
from jax.experimental import pallas as pl
from jax.experimental.pallas import tpu as pltpu
from jax.sharding import PartitionSpec as P

CENTER = 3.0
HALF = 2.5
LANES = 128
ROWS = 8
VMEM_LIMIT = 28 * 1024 * 1024


def pack_kernel(pairs_ref, stored_ref, orbitals_ref, out_ref):
    targets = out_ref.shape[0]
    count = pairs_ref.shape[1]
    stored = stored_ref[...]
    place = lax.broadcasted_iota(jnp.int32, stored.shape, 1).astype(jnp.float32)
    lane = lax.broadcasted_iota(jnp.int32, (ROWS, LANES), 1)
    wanted = jnp.zeros((ROWS, LANES), jnp.float32)
    for half in range(2):
        for pair in range(count):
            hit = stored == pairs_ref[half, pair]
            row = jnp.sum(jnp.where(hit, place, 0.0), axis=1, keepdims=True)
            wanted = jnp.where(lane == half * count + pair, row, wanted)
    bands = orbitals_ref.shape[1]
    wide = orbitals_ref.shape[2] // LANES
    tiles = bands // ROWS * wide
    for target in range(targets):
        if target < tiles:
            group, side = target // wide, target % wide
            tile = orbitals_ref[0, group * ROWS : (group + 1) * ROWS, side * LANES : (side + 1) * LANES]
            tile = tile.astype(jnp.float32)
        else:
            tile = jnp.zeros((ROWS, LANES), jnp.float32)
        out_ref[target] = jnp.concatenate([tile, wanted], axis=0).astype(jnp.bfloat16)


def select_kernel(rows_ref, table_ref, out_ref):
    transfers, count = rows_ref.shape

    def one(transfer, carry):
        for pair in range(count):
            out_ref[transfer * count + pair] = table_ref[rows_ref[transfer, pair], :ROWS, :]
        return carry

    lax.fori_loop(0, transfers, one, 0, unroll=8)


def steps_kernel(pairs_ref, low_ref, high_ref, own_ref, other_ref, start_ref, *refs):
    tiles_w = len(refs) - 10
    pair, column = lax.axis_index("row"), lax.axis_index("col")
    w_refs, out_ref = refs[:tiles_w], refs[tiles_w]
    valence, conduction, w_all, screened_in, screened_out, total, first, flat, sems = refs[tiles_w + 1 :]
    count_v = valence.shape[0]
    count_c = conduction.shape[0]
    points = valence.shape[1]
    rows_w, cols_w = w_refs[0].shape
    wide_w = points // cols_w
    flat_rows = start_ref.shape[0]
    vectors = flat_rows // count_v
    padded = screened_in.shape[0]
    turn = 1 - 2 * column
    steps = (0, -turn, turn, 2, 0, turn, -turn, 2)
    sides = (column,) * 4 + (1 - column,) * 4
    copies = [
        pltpu.make_async_copy(w_refs[t], w_all.at[(pair + steps[t] + 4) % 4 * 2 + sides[t]], sems.at[t])
        for t in range(tiles_w)
    ]
    for copy in copies:
        copy.start()

    even = column == 0
    wide = 2
    row_count = points // (2 * wide * LANES)

    def fetch(tile, block):
        row, core = block // 2, block % 2
        mine = own_ref[tile * row_count + row].astype(jnp.float32)
        theirs = other_ref[tile * row_count + row].astype(jnp.float32)
        return jnp.where(even, mine, theirs) if core == 0 else jnp.where(even, theirs, mine)

    for block in range(2 * row_count):
        for side in range(wide):
            lanes = slice((block * wide + side) * LANES, (block * wide + side + 1) * LANES)
            for pack in range(count_v // (2 * ROWS)):
                tile = [fetch((2 * pack + k) * wide + side, block) for k in range(2)]
                valence[2 * pack * ROWS : 2 * (pack + 1) * ROWS, lanes] = jnp.concatenate(tile, axis=0)
            base = count_v // ROWS
            for pack in range(count_c // (2 * ROWS)):
                tile = [fetch((base + 2 * pack + k) * wide + side, block) for k in range(2)]
                conduction[2 * pack * ROWS : 2 * (pack + 1) * ROWS, lanes] = jnp.concatenate(
                    tile, axis=0
                ).astype(jnp.bfloat16)

    screened_in[...] = jnp.zeros_like(screened_in)

    def kernel_term(current_ref):
        chunk = 512
        def expand(step, carry):
            lanes = pl.ds(pl.multiple_of(step * chunk, chunk), chunk)
            inner = jnp.dot(current_ref[...], conduction[:, lanes], preferred_element_type=jnp.float32)
            inner = inner.reshape(vectors, count_v, chunk) * valence[:, lanes][None]
            screened_in[:vectors, lanes] = jnp.sum(inner, axis=1)
            return carry

        lax.fori_loop(0, points // chunk, expand, 0, unroll=True)
        values = screened_in[...].astype(jnp.bfloat16)
        if current_ref is start_ref:
            for copy in copies:
                copy.wait()
        for row in range(tiles_w // wide_w):
            summed = jnp.zeros((padded, rows_w), jnp.float32)
            for col in range(wide_w):
                summed += lax.dot_general(
                    values[:, col * cols_w : (col + 1) * cols_w],
                    w_all[row * wide_w + col],
                    (((1,), (1,)), ((), ())),
                    preferred_element_type=jnp.float32,
                )
            screened_out[:, row * rows_w : (row + 1) * rows_w] = summed
        total[...] = jnp.zeros_like(total)

        def project(step, carry):
            lanes = pl.ds(pl.multiple_of(step * chunk, chunk), chunk)
            weighted = screened_out[:vectors, lanes][:, None, :] * valence[:, lanes][None]
            weighted = weighted.reshape(flat_rows, chunk).astype(jnp.bfloat16)
            total[...] += lax.dot_general(
                weighted,
                conduction[:, lanes],
                (((1,), (1,)), ((), ())),
                preferred_element_type=jnp.float32,
            )
            return carry

        lax.fori_loop(0, points // chunk, project, 0, unroll=True)

    low = low_ref[pl.ds(pairs_ref[0, pair], 1), :]
    high = high_ref[pl.ds(pairs_ref[1, pair], 1), :]
    square = (count_v, count_v)
    diagonal = lax.broadcasted_iota(jnp.int32, square, 0) == lax.broadcasted_iota(jnp.int32, square, 1)
    low = jnp.sum(jnp.where(diagonal, low, 0.0), axis=1, keepdims=True)
    gap = (high - low)[None]

    def scaled(current):
        parts = current.astype(jnp.float32).reshape(vectors, count_v, count_c)
        term = total[...].reshape(vectors, count_v, count_c)
        return ((gap * parts + term - CENTER * parts) / HALF).reshape(flat_rows, count_c)

    kernel_term(start_ref)
    first[...] = scaled(start_ref[...]).astype(jnp.bfloat16)
    kernel_term(first)
    total[...] = 2.0 * scaled(first[...]) - start_ref[...].astype(jnp.float32)

    quads = flat_rows // 4
    part = [total[pl.ds(k, quads, stride=4), :] for k in range(4)]
    third = LANES - count_c
    flat[pl.ds(0, quads, stride=3), :] = jnp.concatenate([part[0], part[1][:, :third]], axis=1)
    flat[pl.ds(1, quads, stride=3), :] = jnp.concatenate([part[1][:, third:], part[2][:, : 2 * third]], axis=1)
    flat[pl.ds(2, quads, stride=3), :] = jnp.concatenate([part[2][:, 2 * third :], part[3]], axis=1)
    out_ref[...] = flat[...].astype(jnp.bfloat16)


def on_device(amplitudes, pairs, stored_k, orbitals, valence_energy, conduction_energy, screened):
    transfers = stored_k.shape[0]
    count_v = valence_energy.shape[1]
    count_c = conduction_energy.shape[1]
    vectors, pair_count, flat_size = amplitudes.shape[1:]
    member = lax.axis_index("pb")
    pair = lax.axis_index("row")
    column = lax.axis_index("col")
    rows_axis, cols = lax.axis_size("row"), lax.axis_size("col")
    devices = rows_axis * cols
    points = orbitals.shape[2] * devices
    share = vectors // cols
    flat_rows = share * count_v
    padded = 16
    smem = pl.BlockSpec(memory_space=pltpu.SMEM)
    vmem = pl.BlockSpec(memory_space=pltpu.VMEM)
    anywhere = pl.BlockSpec(memory_space=pl.ANY)
    limit = pltpu.CompilerParams(vmem_limit_bytes=VMEM_LIMIT)
    swap = [(0, 1), (1, 0)]
    ring = [(r, c) for r in range(rows_axis) for c in range(cols)]
    there = [(r * cols + c, (r + 1 - 2 * c) % rows_axis * cols + c) for r, c in ring]
    back = [(target, source) for source, target in there]

    wishes = pairs[0].T
    message = pl.pallas_call(
        pack_kernel,
        out_shape=jax.ShapeDtypeStruct((transfers, 2 * ROWS, LANES), jnp.bfloat16),
        in_specs=[smem, vmem, vmem],
        out_specs=vmem,
        compiler_params=limit,
    )(wishes, stored_k.reshape(1, transfers), orbitals)
    table = lax.all_to_all(message, "pb", 0, 0, tiled=True)

    start = lax.dynamic_slice(
        amplitudes[0],
        (column * share, pair, 0),
        (share, 1, flat_size),
        allow_negative_indices=False,
    ).reshape(flat_rows, count_c)
    w_own, _ = lax.optimization_barrier((screened[0], message))
    w_there = lax.ppermute(w_own, ("row", "col"), there)
    w_back = lax.ppermute(w_own, ("row", "col"), back)

    w_far = lax.ppermute(w_there, ("row", "col"), there)
    table, start = lax.optimization_barrier((table, start))

    wanted = table[:, ROWS, : 2 * pair_count].astype(jnp.int32)
    valence_tiles = count_v // ROWS * (orbitals.shape[2] // LANES)
    rows = jnp.where(member < valence_tiles, wanted[:, :pair_count], wanted[:, pair_count:])
    chosen = pl.pallas_call(
        select_kernel,
        out_shape=jax.ShapeDtypeStruct((transfers * pair_count, ROWS, LANES), jnp.bfloat16),
        in_specs=[smem, vmem],
        out_specs=vmem,
        compiler_params=limit,
    )(rows, table)
    own = lax.all_to_all(chosen, ("pb", "row"), 0, 0, tiled=True)

    w_core = [w_own, w_there, w_back, w_far]
    w_tiles = w_core + [lax.ppermute(tile, "col", swap) for tile in w_core]
    other = lax.ppermute(own, "col", swap)

    result = pl.pallas_call(
        steps_kernel,
        out_shape=jax.ShapeDtypeStruct((flat_rows * count_c // LANES, LANES), jnp.bfloat16),
        in_specs=[smem, vmem, vmem, vmem, vmem, vmem] + [anywhere] * devices,
        out_specs=vmem,
        scratch_shapes=[
            pltpu.VMEM((count_v, points), jnp.float32),
            pltpu.VMEM((count_c, points), jnp.bfloat16),
            pltpu.VMEM((devices,) + screened.shape[1:], jnp.bfloat16),
            pltpu.VMEM((padded, points), jnp.float32),
            pltpu.VMEM((padded, points), jnp.float32),
            pltpu.VMEM((flat_rows, count_c), jnp.float32),
            pltpu.VMEM((flat_rows, count_c), jnp.bfloat16),
            pltpu.VMEM((flat_rows * count_c // LANES, LANES), jnp.float32),
            pltpu.SemaphoreType.DMA((devices,)),
        ],
        compiler_params=limit,
    )(wishes, valence_energy, conduction_energy, own, other, start, *w_tiles)

    mine = result.reshape(share, flat_size // LANES, LANES)
    across = lax.all_gather(mine, "row")
    theirs = lax.ppermute(across, "col", swap)
    both = jnp.where(column == 0, jnp.stack([across, theirs]), jnp.stack([theirs, across]))
    return both.transpose(0, 2, 1, 3, 4).reshape(1, vectors, pair_count, flat_size)


def solution(mesh):
    return jax.shard_map(
        on_device,
        mesh=mesh,
        in_specs=(
            P("pb", None, None, None),
            P("pb", None, None),
            P(),
            P("pb", None, ("row", "col")),
            P(),
            P(),
            P("pb", "row", "col"),
        ),
        out_specs=P("pb", None, None, None),
        check_vma=False,
    )
```

```python
import jax
import jax.numpy as jnp
from jax import lax
from jax.experimental import pallas as pl
from jax.experimental.pallas import tpu as pltpu
from jax.sharding import PartitionSpec as P

CENTER = 3.0
HALF = 2.5
LANES = 128
ROWS = 8
QUAD = 4
PARTS = 3
VMEM_LIMIT = 28 * 1024 * 1024


def piece_of(slot, part):
    tile = slot // QUAD * PARTS + part
    return tile, slot % QUAD


def pack_kernel(pairs_ref, stored_ref, orbitals_ref, out_ref):
    targets = out_ref.shape[0]
    count = pairs_ref.shape[1]
    stored = stored_ref[...]
    place = lax.broadcasted_iota(jnp.int32, stored.shape, 1).astype(jnp.float32)
    lane = lax.broadcasted_iota(jnp.int32, (2, LANES), 1)
    wanted = jnp.zeros((2, LANES), jnp.float32)
    for half in range(2):
        for pair in range(count):
            hit = stored == pairs_ref[half, pair]
            row = jnp.sum(jnp.where(hit, place, 0.0), axis=1, keepdims=True)
            wanted = jnp.where(lane == half * count + pair, row, wanted)
    bands = orbitals_ref.shape[1]
    wide = orbitals_ref.shape[2] // LANES
    own = orbitals_ref[0].astype(jnp.float32)
    for target in range(targets):
        half, slot = divmod(target, targets // 2)
        parts = []
        for part in range(PARTS):
            tile, quarter = piece_of(slot, part)
            row = half * (bands // 2) + tile // wide * ROWS + 2 * quarter
            side = tile % wide
            parts.append(own[row : row + 2, side * LANES : (side + 1) * LANES])
        out_ref[target] = jnp.concatenate(parts + [wanted], axis=1).astype(jnp.bfloat16)


def select_kernel(rows_ref, table_ref, out_ref):
    transfers, count = rows_ref.shape
    width = out_ref.shape[2]

    def one(transfer, carry):
        for pair in range(count):
            out_ref[transfer * count + pair] = table_ref[rows_ref[transfer, pair], :, :width]
        return carry

    lax.fori_loop(0, transfers, one, 0, unroll=8)


def steps_kernel(pairs_ref, low_ref, high_ref, own_ref, other_ref, start_ref, *refs):
    tiles_w = len(refs) - 10
    pair, column = lax.axis_index("row"), lax.axis_index("col")
    w_refs, out_ref = refs[:tiles_w], refs[tiles_w]
    valence, conduction, w_all, screened_in, screened_out, total, first, flat, sems = refs[tiles_w + 1 :]
    count_v = valence.shape[0]
    count_c = conduction.shape[0]
    points = valence.shape[1]
    rows_w, cols_w = w_refs[0].shape
    wide_w = points // cols_w
    flat_rows = start_ref.shape[0]
    vectors = flat_rows // count_v
    padded = screened_in.shape[0]
    turn = 1 - 2 * column
    steps = (0, -turn, turn, 2, 0, turn, -turn, 2)
    sides = (column,) * 4 + (1 - column,) * 4
    copies = [
        pltpu.make_async_copy(w_refs[t], w_all.at[(pair + steps[t] + 4) % 4 * 2 + sides[t]], sems.at[t])
        for t in range(tiles_w)
    ]
    for copy in copies:
        copy.start()

    wide = 2
    row_count = points // (2 * wide * LANES)
    tiles = count_v // ROWS * wide
    slots = tiles // PARTS * QUAD

    def assemble(cores):
        def fetch(tile, block):
            half, tile = divmod(tile, tiles)
            part = tile % PARTS
            first = half * slots + tile // PARTS * QUAD
            lanes = slice(part * LANES, (part + 1) * LANES)
            rows = [cores[block % 2][(first + k) * row_count + block // 2, :, lanes] for k in range(QUAD)]
            return jnp.concatenate([row.astype(jnp.float32) for row in rows], axis=0)

        for block in range(2 * row_count):
            for side in range(wide):
                lanes = slice((block * wide + side) * LANES, (block * wide + side + 1) * LANES)
                for pack in range(count_v // (2 * ROWS)):
                    pair_of = [fetch((2 * pack + k) * wide + side, block) for k in range(2)]
                    valence[2 * pack * ROWS : 2 * (pack + 1) * ROWS, lanes] = jnp.concatenate(pair_of, axis=0)
                base = count_v // ROWS
                for pack in range(count_c // (2 * ROWS)):
                    pair_of = [fetch((base + 2 * pack + k) * wide + side, block) for k in range(2)]
                    conduction[2 * pack * ROWS : 2 * (pack + 1) * ROWS, lanes] = jnp.concatenate(
                        pair_of, axis=0
                    ).astype(jnp.bfloat16)

    @pl.when(column == 0)
    def _():
        assemble((own_ref, other_ref))

    @pl.when(column == 1)
    def _():
        assemble((other_ref, own_ref))

    screened_in[...] = jnp.zeros_like(screened_in)

    def kernel_term(current_ref):
        chunk = 512
        def expand(step, carry):
            lanes = pl.ds(pl.multiple_of(step * chunk, chunk), chunk)
            inner = jnp.dot(current_ref[...], conduction[:, lanes], preferred_element_type=jnp.float32)
            inner = inner.reshape(vectors, count_v, chunk) * valence[:, lanes][None]
            screened_in[:vectors, lanes] = jnp.sum(inner, axis=1)
            return carry

        lax.fori_loop(0, points // chunk, expand, 0, unroll=True)
        values = screened_in[...].astype(jnp.bfloat16)
        if current_ref is start_ref:
            for copy in copies:
                copy.wait()
        for row in range(tiles_w // wide_w):
            summed = jnp.zeros((padded, rows_w), jnp.float32)
            for col in range(wide_w):
                summed += lax.dot_general(
                    values[:, col * cols_w : (col + 1) * cols_w],
                    w_all[row * wide_w + col],
                    (((1,), (1,)), ((), ())),
                    preferred_element_type=jnp.float32,
                )
            screened_out[:, row * rows_w : (row + 1) * rows_w] = summed
        total[...] = jnp.zeros_like(total)

        def project(step, carry):
            lanes = pl.ds(pl.multiple_of(step * chunk, chunk), chunk)
            weighted = screened_out[:vectors, lanes][:, None, :] * valence[:, lanes][None]
            weighted = weighted.reshape(flat_rows, chunk).astype(jnp.bfloat16)
            total[...] += lax.dot_general(
                weighted,
                conduction[:, lanes],
                (((1,), (1,)), ((), ())),
                preferred_element_type=jnp.float32,
            )
            return carry

        lax.fori_loop(0, points // chunk, project, 0, unroll=True)

    low = low_ref[pl.ds(pairs_ref[0, pair], 1), :]
    high = high_ref[pl.ds(pairs_ref[1, pair], 1), :]
    square = (count_v, count_v)
    diagonal = lax.broadcasted_iota(jnp.int32, square, 0) == lax.broadcasted_iota(jnp.int32, square, 1)
    low = jnp.sum(jnp.where(diagonal, low, 0.0), axis=1, keepdims=True)
    gap = (high - low)[None]

    def scaled(current):
        parts = current.astype(jnp.float32).reshape(vectors, count_v, count_c)
        term = total[...].reshape(vectors, count_v, count_c)
        return ((gap * parts + term - CENTER * parts) / HALF).reshape(flat_rows, count_c)

    kernel_term(start_ref)
    first[...] = scaled(start_ref[...]).astype(jnp.bfloat16)
    kernel_term(first)
    total[...] = 2.0 * scaled(first[...]) - start_ref[...].astype(jnp.float32)

    quads = flat_rows // 4
    part = [total[pl.ds(k, quads, stride=4), :] for k in range(4)]
    third = LANES - count_c
    flat[pl.ds(0, quads, stride=3), :] = jnp.concatenate([part[0], part[1][:, :third]], axis=1)
    flat[pl.ds(1, quads, stride=3), :] = jnp.concatenate([part[1][:, third:], part[2][:, : 2 * third]], axis=1)
    flat[pl.ds(2, quads, stride=3), :] = jnp.concatenate([part[2][:, 2 * third :], part[3]], axis=1)
    out_ref[...] = flat[...].astype(jnp.bfloat16)


def on_device(amplitudes, pairs, stored_k, orbitals, valence_energy, conduction_energy, screened):
    transfers = stored_k.shape[0]
    count_v = valence_energy.shape[1]
    count_c = conduction_energy.shape[1]
    vectors, pair_count, flat_size = amplitudes.shape[1:]
    member = lax.axis_index("pb")
    pair = lax.axis_index("row")
    column = lax.axis_index("col")
    rows_axis, cols = lax.axis_size("row"), lax.axis_size("col")
    devices = rows_axis * cols
    points = orbitals.shape[2] * devices
    share = vectors // cols
    flat_rows = share * count_v
    padded = 16
    smem = pl.BlockSpec(memory_space=pltpu.SMEM)
    vmem = pl.BlockSpec(memory_space=pltpu.VMEM)
    anywhere = pl.BlockSpec(memory_space=pl.ANY)
    limit = pltpu.CompilerParams(vmem_limit_bytes=VMEM_LIMIT)
    width = PARTS * LANES
    swap = [(0, 1), (1, 0)]
    ring = [(r, c) for r in range(rows_axis) for c in range(cols)]
    there = [(r * cols + c, (r + 1 - 2 * c) % rows_axis * cols + c) for r, c in ring]
    back = [(target, source) for source, target in there]

    wishes = pairs[0].T
    message = pl.pallas_call(
        pack_kernel,
        out_shape=jax.ShapeDtypeStruct((transfers, 2, width + LANES), jnp.bfloat16),
        in_specs=[smem, vmem, vmem],
        out_specs=vmem,
        compiler_params=pltpu.CompilerParams(vmem_limit_bytes=2 * VMEM_LIMIT),
    )(wishes, stored_k.reshape(1, transfers), orbitals)
    table = lax.all_to_all(message, "pb", 0, 0, tiled=True)

    start = lax.dynamic_slice(
        amplitudes[0],
        (column * share, pair, 0),
        (share, 1, flat_size),
        allow_negative_indices=False,
    ).reshape(flat_rows, count_c)
    w_own, _ = lax.optimization_barrier((screened[0], message))
    w_there = lax.ppermute(w_own, ("row", "col"), there)
    w_back = lax.ppermute(w_own, ("row", "col"), back)

    table, start = lax.optimization_barrier((table, start))
    w_next, _ = lax.optimization_barrier((w_there, table))
    w_far = lax.ppermute(w_next, ("row", "col"), there)

    wanted = table[:, 0, width : width + 2 * pair_count].astype(jnp.int32)
    rows = jnp.where(member < transfers // 2, wanted[:, :pair_count], wanted[:, pair_count:])
    chosen = pl.pallas_call(
        select_kernel,
        out_shape=jax.ShapeDtypeStruct((transfers * pair_count, 2, width), jnp.bfloat16),
        in_specs=[smem, vmem],
        out_specs=vmem,
        compiler_params=limit,
    )(rows, table)
    own = lax.all_to_all(chosen, ("pb", "row"), 0, 0, tiled=True)

    w_core = [w_own, w_there, w_back, w_far]
    w_tiles = w_core + [lax.ppermute(tile, "col", swap) for tile in w_core]
    other = lax.ppermute(own, "col", swap)

    result = pl.pallas_call(
        steps_kernel,
        out_shape=jax.ShapeDtypeStruct((flat_rows * count_c // LANES, LANES), jnp.bfloat16),
        in_specs=[smem, vmem, vmem, vmem, vmem, vmem] + [anywhere] * devices,
        out_specs=vmem,
        scratch_shapes=[
            pltpu.VMEM((count_v, points), jnp.float32),
            pltpu.VMEM((count_c, points), jnp.bfloat16),
            pltpu.VMEM((devices,) + screened.shape[1:], jnp.bfloat16),
            pltpu.VMEM((padded, points), jnp.float32),
            pltpu.VMEM((padded, points), jnp.float32),
            pltpu.VMEM((flat_rows, count_c), jnp.float32),
            pltpu.VMEM((flat_rows, count_c), jnp.bfloat16),
            pltpu.VMEM((flat_rows * count_c // LANES, LANES), jnp.float32),
            pltpu.SemaphoreType.DMA((devices,)),
        ],
        compiler_params=limit,
    )(wishes, valence_energy, conduction_energy, own, other, start, *w_tiles)

    mine = result.reshape(share, flat_size // LANES, LANES)
    across = lax.all_gather(mine, "row")
    theirs = lax.ppermute(across, "col", swap)
    both = jnp.where(column == 0, jnp.stack([across, theirs]), jnp.stack([theirs, across]))
    return both.transpose(0, 2, 1, 3, 4).reshape(1, vectors, pair_count, flat_size)


def solution(mesh):
    return jax.shard_map(
        on_device,
        mesh=mesh,
        in_specs=(
            P("pb", None, None, None),
            P("pb", None, None),
            P(),
            P("pb", None, ("row", "col")),
            P(),
            P(),
            P("pb", "row", "col"),
        ),
        out_specs=P("pb", None, None, None),
        check_vma=False,
    )
```

```python
import jax
import jax.numpy as jnp
from jax import lax
from jax.experimental import pallas as pl
from jax.experimental.pallas import tpu as pltpu
from jax.sharding import PartitionSpec as P

CENTER = 3.0
HALF = 2.5
LANES = 128
ROWS = 8
QUAD = 4
PARTS = 3
VMEM_LIMIT = 28 * 1024 * 1024


def piece_of(slot, part):
    tile = slot // QUAD * PARTS + part
    return tile, slot % QUAD


def pack_kernel(pairs_ref, stored_ref, orbitals_ref, out_ref):
    targets = out_ref.shape[0]
    count = pairs_ref.shape[1]
    stored = stored_ref[...]
    place = lax.broadcasted_iota(jnp.int32, stored.shape, 1).astype(jnp.float32)
    lane = lax.broadcasted_iota(jnp.int32, (2, LANES), 1)
    wanted = jnp.zeros((2, LANES), jnp.float32)
    for half in range(2):
        for pair in range(count):
            hit = stored == pairs_ref[half, pair]
            row = jnp.sum(jnp.where(hit, place, 0.0), axis=1, keepdims=True)
            wanted = jnp.where(lane == half * count + pair, row, wanted)
    bands = orbitals_ref.shape[1]
    wide = orbitals_ref.shape[2] // LANES
    own = orbitals_ref[0].astype(jnp.float32)
    for target in range(targets):
        half, slot = divmod(target, targets // 2)
        parts = []
        for part in range(PARTS):
            tile, quarter = piece_of(slot, part)
            row = half * (bands // 2) + tile // wide * ROWS + 2 * quarter
            side = tile % wide
            parts.append(own[row : row + 2, side * LANES : (side + 1) * LANES])
        out_ref[target] = jnp.concatenate(parts + [wanted], axis=1).astype(jnp.bfloat16)


def select_kernel(rows_ref, table_ref, out_ref):
    transfers = rows_ref.shape[0]
    count = rows_ref.shape[1] // 2
    width = out_ref.shape[2]
    first = jnp.where(lax.axis_index("pb") < transfers // 2, 0, count)

    def one(transfer, carry):
        for pair in range(count):
            out_ref[transfer * count + pair] = table_ref[rows_ref[transfer, first + pair], :, :width]
        return carry

    lax.fori_loop(0, transfers, one, 0, unroll=8)


def steps_kernel(pairs_ref, low_ref, high_ref, own_ref, other_ref, start_ref, *refs):
    tiles_w = len(refs) - 10
    pair, column = lax.axis_index("row"), lax.axis_index("col")
    w_refs, out_ref = refs[:tiles_w], refs[tiles_w]
    valence, conduction, w_all, screened_in, screened_out, total, first, flat, sems = refs[tiles_w + 1 :]
    count_v = valence.shape[0]
    count_c = conduction.shape[0]
    points = valence.shape[1]
    rows_w, cols_w = w_refs[0].shape
    wide_w = points // cols_w
    flat_rows = start_ref.shape[0]
    vectors = flat_rows // count_v
    padded = screened_in.shape[0]
    turn = 1 - 2 * column
    steps = (0, -turn, turn, 2, 0, turn, -turn, 2)
    sides = (column,) * 4 + (1 - column,) * 4
    copies = [
        pltpu.make_async_copy(w_refs[t], w_all.at[(pair + steps[t] + 4) % 4 * 2 + sides[t]], sems.at[t])
        for t in range(tiles_w)
    ]
    for copy in copies:
        copy.start()

    wide = 2
    row_count = points // (2 * wide * LANES)
    tiles = count_v // ROWS * wide
    slots = tiles // PARTS * QUAD

    def assemble(cores):
        def fetch(tile, block):
            half, tile = divmod(tile, tiles)
            part = tile % PARTS
            first = half * slots + tile // PARTS * QUAD
            lanes = slice(part * LANES, (part + 1) * LANES)
            rows = [cores[block % 2][(first + k) * row_count + block // 2, :, lanes] for k in range(QUAD)]
            return jnp.concatenate([row.astype(jnp.float32) for row in rows], axis=0)

        for block in range(2 * row_count):
            for side in range(wide):
                lanes = slice((block * wide + side) * LANES, (block * wide + side + 1) * LANES)
                for pack in range(count_v // (2 * ROWS)):
                    pair_of = [fetch((2 * pack + k) * wide + side, block) for k in range(2)]
                    valence[2 * pack * ROWS : 2 * (pack + 1) * ROWS, lanes] = jnp.concatenate(pair_of, axis=0)
                base = count_v // ROWS
                for pack in range(count_c // (2 * ROWS)):
                    pair_of = [fetch((base + 2 * pack + k) * wide + side, block) for k in range(2)]
                    conduction[2 * pack * ROWS : 2 * (pack + 1) * ROWS, lanes] = jnp.concatenate(
                        pair_of, axis=0
                    ).astype(jnp.bfloat16)

    @pl.when(column == 0)
    def _():
        assemble((own_ref, other_ref))

    @pl.when(column == 1)
    def _():
        assemble((other_ref, own_ref))

    screened_in[...] = jnp.zeros_like(screened_in)

    def kernel_term(current_ref):
        chunk = 512
        def expand(step, carry):
            lanes = pl.ds(pl.multiple_of(step * chunk, chunk), chunk)
            inner = jnp.dot(current_ref[...], conduction[:, lanes], preferred_element_type=jnp.float32)
            inner = inner.reshape(vectors, count_v, chunk) * valence[:, lanes][None]
            screened_in[:vectors, lanes] = jnp.sum(inner, axis=1)
            return carry

        lax.fori_loop(0, points // chunk, expand, 0, unroll=True)
        values = screened_in[...].astype(jnp.bfloat16)
        if current_ref is start_ref:
            for copy in copies:
                copy.wait()
        for row in range(tiles_w // wide_w):
            summed = jnp.zeros((padded, rows_w), jnp.float32)
            for col in range(wide_w):
                summed += lax.dot_general(
                    values[:, col * cols_w : (col + 1) * cols_w],
                    w_all[row * wide_w + col],
                    (((1,), (1,)), ((), ())),
                    preferred_element_type=jnp.float32,
                )
            screened_out[:, row * rows_w : (row + 1) * rows_w] = summed
        total[...] = jnp.zeros_like(total)

        def project(step, carry):
            lanes = pl.ds(pl.multiple_of(step * chunk, chunk), chunk)
            weighted = screened_out[:vectors, lanes][:, None, :] * valence[:, lanes][None]
            weighted = weighted.reshape(flat_rows, chunk).astype(jnp.bfloat16)
            total[...] += lax.dot_general(
                weighted,
                conduction[:, lanes],
                (((1,), (1,)), ((), ())),
                preferred_element_type=jnp.float32,
            )
            return carry

        lax.fori_loop(0, points // chunk, project, 0, unroll=True)

    low = low_ref[pl.ds(pairs_ref[0, pair], 1), :]
    high = high_ref[pl.ds(pairs_ref[1, pair], 1), :]
    square = (count_v, count_v)
    diagonal = lax.broadcasted_iota(jnp.int32, square, 0) == lax.broadcasted_iota(jnp.int32, square, 1)
    low = jnp.sum(jnp.where(diagonal, low, 0.0), axis=1, keepdims=True)
    gap = (high - low)[None]

    def scaled(current):
        parts = current.astype(jnp.float32).reshape(vectors, count_v, count_c)
        term = total[...].reshape(vectors, count_v, count_c)
        return ((gap * parts + term - CENTER * parts) / HALF).reshape(flat_rows, count_c)

    kernel_term(start_ref)
    first[...] = scaled(start_ref[...]).astype(jnp.bfloat16)
    kernel_term(first)
    total[...] = 2.0 * scaled(first[...]) - start_ref[...].astype(jnp.float32)

    quads = flat_rows // 4
    part = [total[pl.ds(k, quads, stride=4), :] for k in range(4)]
    third = LANES - count_c
    flat[pl.ds(0, quads, stride=3), :] = jnp.concatenate([part[0], part[1][:, :third]], axis=1)
    flat[pl.ds(1, quads, stride=3), :] = jnp.concatenate([part[1][:, third:], part[2][:, : 2 * third]], axis=1)
    flat[pl.ds(2, quads, stride=3), :] = jnp.concatenate([part[2][:, 2 * third :], part[3]], axis=1)
    out_ref[...] = flat[...].astype(jnp.bfloat16)


def on_device(amplitudes, pairs, stored_k, orbitals, valence_energy, conduction_energy, screened):
    transfers = stored_k.shape[0]
    count_v = valence_energy.shape[1]
    count_c = conduction_energy.shape[1]
    vectors, pair_count, flat_size = amplitudes.shape[1:]
    pair = lax.axis_index("row")
    column = lax.axis_index("col")
    rows_axis, cols = lax.axis_size("row"), lax.axis_size("col")
    devices = rows_axis * cols
    points = orbitals.shape[2] * devices
    share = vectors // cols
    flat_rows = share * count_v
    padded = 16
    smem = pl.BlockSpec(memory_space=pltpu.SMEM)
    vmem = pl.BlockSpec(memory_space=pltpu.VMEM)
    anywhere = pl.BlockSpec(memory_space=pl.ANY)
    limit = pltpu.CompilerParams(vmem_limit_bytes=VMEM_LIMIT)
    width = PARTS * LANES
    swap = [(0, 1), (1, 0)]
    ring = [(r, c) for r in range(rows_axis) for c in range(cols)]
    there = [(r * cols + c, (r + 1 - 2 * c) % rows_axis * cols + c) for r, c in ring]
    back = [(target, source) for source, target in there]

    wishes = pairs[0].T
    message = pl.pallas_call(
        pack_kernel,
        out_shape=jax.ShapeDtypeStruct((transfers, 2, width + LANES), jnp.bfloat16),
        in_specs=[smem, vmem, vmem],
        out_specs=vmem,
        compiler_params=pltpu.CompilerParams(vmem_limit_bytes=2 * VMEM_LIMIT),
    )(wishes, stored_k.reshape(1, transfers), orbitals)
    table = lax.all_to_all(message, "pb", 0, 0, tiled=True)

    start = lax.dynamic_slice(
        amplitudes[0],
        (column * share, pair, 0),
        (share, 1, flat_size),
        allow_negative_indices=False,
    ).reshape(flat_rows, count_c)
    w_own, _ = lax.optimization_barrier((screened[0], message))
    w_there = lax.ppermute(w_own, ("row", "col"), there)
    w_back = lax.ppermute(w_own, ("row", "col"), back)

    w_far = lax.ppermute(w_there, ("row", "col"), there)
    table, start = lax.optimization_barrier((table, start))

    wanted = table[:, 0, width : width + 2 * pair_count].astype(jnp.int32)
    chosen = pl.pallas_call(
        select_kernel,
        out_shape=jax.ShapeDtypeStruct((transfers * pair_count, 2, width), jnp.bfloat16),
        in_specs=[smem, vmem],
        out_specs=vmem,
        compiler_params=limit,
    )(wanted, table)
    own = lax.all_to_all(chosen, ("pb", "row"), 0, 0, tiled=True)

    other = lax.ppermute(own, "col", swap)
    w_last, _ = lax.optimization_barrier((w_far, own))
    w_core = [w_own, w_there, w_back, w_last]
    w_tiles = w_core + [lax.ppermute(tile, "col", swap) for tile in w_core]

    result = pl.pallas_call(
        steps_kernel,
        out_shape=jax.ShapeDtypeStruct((flat_rows * count_c // LANES, LANES), jnp.bfloat16),
        in_specs=[smem, vmem, vmem, vmem, vmem, vmem] + [anywhere] * devices,
        out_specs=vmem,
        scratch_shapes=[
            pltpu.VMEM((count_v, points), jnp.float32),
            pltpu.VMEM((count_c, points), jnp.bfloat16),
            pltpu.VMEM((devices,) + screened.shape[1:], jnp.bfloat16),
            pltpu.VMEM((padded, points), jnp.float32),
            pltpu.VMEM((padded, points), jnp.float32),
            pltpu.VMEM((flat_rows, count_c), jnp.float32),
            pltpu.VMEM((flat_rows, count_c), jnp.bfloat16),
            pltpu.VMEM((flat_rows * count_c // LANES, LANES), jnp.float32),
            pltpu.SemaphoreType.DMA((devices,)),
        ],
        compiler_params=limit,
    )(wishes, valence_energy, conduction_energy, own, other, start, *w_tiles)

    mine = result.reshape(share, flat_size // LANES, LANES)
    across = lax.all_gather(mine, "row")
    theirs = lax.ppermute(across, "col", swap)
    both = jnp.where(column == 0, jnp.stack([across, theirs]), jnp.stack([theirs, across]))
    return both.transpose(0, 2, 1, 3, 4).reshape(1, vectors, pair_count, flat_size)


def solution(mesh):
    return jax.shard_map(
        on_device,
        mesh=mesh,
        in_specs=(
            P("pb", None, None, None),
            P("pb", None, None),
            P(),
            P("pb", None, ("row", "col")),
            P(),
            P(),
            P("pb", "row", "col"),
        ),
        out_specs=P("pb", None, None, None),
        check_vma=False,
    )
```

```python
import jax
import jax.numpy as jnp
from jax import lax
from jax.experimental import pallas as pl
from jax.experimental.pallas import tpu as pltpu
from jax.sharding import PartitionSpec as P

CENTER = 3.0
HALF = 2.5
LANES = 128
ROWS = 8
QUAD = 4
PARTS = 3
VMEM_LIMIT = 28 * 1024 * 1024


def piece_of(slot, part):
    tile = slot // QUAD * PARTS + part
    return tile, slot % QUAD


def pack_kernel(pairs_ref, stored_ref, orbitals_ref, out_ref):
    targets = out_ref.shape[0]
    count = pairs_ref.shape[1]
    stored = stored_ref[...]
    place = lax.broadcasted_iota(jnp.int32, stored.shape, 1).astype(jnp.float32)
    lane = lax.broadcasted_iota(jnp.int32, (2, LANES), 1)
    wanted = jnp.zeros((2, LANES), jnp.float32)
    for half in range(2):
        for pair in range(count):
            hit = stored == pairs_ref[half, pair]
            row = jnp.sum(jnp.where(hit, place, 0.0), axis=1, keepdims=True)
            wanted = jnp.where(lane == half * count + pair, row, wanted)
    bands = orbitals_ref.shape[1]
    wide = orbitals_ref.shape[2] // LANES
    own = orbitals_ref[0].astype(jnp.float32)
    for target in range(targets):
        half, slot = divmod(target, targets // 2)
        parts = []
        for part in range(PARTS):
            tile, quarter = piece_of(slot, part)
            row = half * (bands // 2) + tile // wide * ROWS + 2 * quarter
            side = tile % wide
            parts.append(own[row : row + 2, side * LANES : (side + 1) * LANES])
        out_ref[target] = jnp.concatenate(parts + [wanted], axis=1).astype(jnp.bfloat16)


def select_kernel(rows_ref, table_ref, out_ref):
    transfers = rows_ref.shape[0]
    count = rows_ref.shape[1] // 2
    width = out_ref.shape[2]
    first = jnp.where(lax.axis_index("pb") < transfers // 2, 0, count)

    def one(transfer, carry):
        for pair in range(count):
            out_ref[transfer * count + pair] = table_ref[rows_ref[transfer, first + pair], :, :width]
        return carry

    lax.fori_loop(0, transfers, one, 0, unroll=8)


def steps_kernel(pairs_ref, low_ref, high_ref, own_ref, other_ref, start_ref, *refs):
    tiles_w = len(refs) - 10
    pair, column = lax.axis_index("row"), lax.axis_index("col")
    w_refs, out_ref = refs[:tiles_w], refs[tiles_w]
    valence, conduction, w_all, screened_in, screened_out, total, first, flat, sems = refs[tiles_w + 1 :]
    count_v = valence.shape[0]
    count_c = conduction.shape[0]
    points = valence.shape[1]
    rows_w, cols_w = w_refs[0].shape
    wide_w = points // cols_w
    flat_rows = start_ref.shape[0]
    vectors = flat_rows // count_v
    padded = screened_in.shape[0]
    turn = 1 - 2 * column
    steps = (0, -turn, turn, 2, 0, turn, -turn, 2)
    sides = (column,) * 4 + (1 - column,) * 4
    copies = [
        pltpu.make_async_copy(w_refs[t], w_all.at[(pair + steps[t] + 4) % 4 * 2 + sides[t]], sems.at[t])
        for t in range(tiles_w)
    ]
    for copy in copies:
        copy.start()

    wide = 2
    row_count = points // (2 * wide * LANES)
    tiles = count_v // ROWS * wide
    slots = tiles // PARTS * QUAD

    def assemble(cores):
        def fetch(tile, block):
            half, tile = divmod(tile, tiles)
            part = tile % PARTS
            first = half * slots + tile // PARTS * QUAD
            lanes = slice(part * LANES, (part + 1) * LANES)
            rows = [cores[block % 2][(first + k) * row_count + block // 2, :, lanes] for k in range(QUAD)]
            return jnp.concatenate([row.astype(jnp.float32) for row in rows], axis=0)

        for block in range(2 * row_count):
            for side in range(wide):
                lanes = slice((block * wide + side) * LANES, (block * wide + side + 1) * LANES)
                for pack in range(count_v // (2 * ROWS)):
                    pair_of = [fetch((2 * pack + k) * wide + side, block) for k in range(2)]
                    valence[2 * pack * ROWS : 2 * (pack + 1) * ROWS, lanes] = jnp.concatenate(pair_of, axis=0)
                base = count_v // ROWS
                for pack in range(count_c // (2 * ROWS)):
                    pair_of = [fetch((base + 2 * pack + k) * wide + side, block) for k in range(2)]
                    conduction[2 * pack * ROWS : 2 * (pack + 1) * ROWS, lanes] = jnp.concatenate(
                        pair_of, axis=0
                    ).astype(jnp.bfloat16)

    @pl.when(column == 0)
    def _():
        assemble((own_ref, other_ref))

    @pl.when(column == 1)
    def _():
        assemble((other_ref, own_ref))

    screened_in[...] = jnp.zeros_like(screened_in)

    def kernel_term(current_ref):
        chunk = 512
        def expand(step, carry):
            lanes = pl.ds(pl.multiple_of(step * chunk, chunk), chunk)
            inner = jnp.dot(current_ref[...], conduction[:, lanes], preferred_element_type=jnp.float32)
            inner = inner.reshape(vectors, count_v, chunk) * valence[:, lanes][None]
            screened_in[:vectors, lanes] = jnp.sum(inner, axis=1)
            return carry

        lax.fori_loop(0, points // chunk, expand, 0, unroll=True)
        values = screened_in[...].astype(jnp.bfloat16)
        if current_ref is start_ref:
            for copy in copies:
                copy.wait()
        for row in range(tiles_w // wide_w):
            summed = jnp.zeros((padded, rows_w), jnp.float32)
            for col in range(wide_w):
                summed += lax.dot_general(
                    values[:, col * cols_w : (col + 1) * cols_w],
                    w_all[row * wide_w + col],
                    (((1,), (1,)), ((), ())),
                    preferred_element_type=jnp.float32,
                )
            screened_out[:, row * rows_w : (row + 1) * rows_w] = summed
        total[...] = jnp.zeros_like(total)

        def project(step, carry):
            lanes = pl.ds(pl.multiple_of(step * chunk, chunk), chunk)
            weighted = screened_out[:vectors, lanes][:, None, :] * valence[:, lanes][None]
            weighted = weighted.reshape(flat_rows, chunk).astype(jnp.bfloat16)
            total[...] += lax.dot_general(
                weighted,
                conduction[:, lanes],
                (((1,), (1,)), ((), ())),
                preferred_element_type=jnp.float32,
            )
            return carry

        lax.fori_loop(0, points // chunk, project, 0, unroll=True)

    low = low_ref[pl.ds(pairs_ref[0, pair], 1), :]
    high = high_ref[pl.ds(pairs_ref[1, pair], 1), :]
    square = (count_v, count_v)
    diagonal = lax.broadcasted_iota(jnp.int32, square, 0) == lax.broadcasted_iota(jnp.int32, square, 1)
    low = jnp.sum(jnp.where(diagonal, low, 0.0), axis=1, keepdims=True)
    gap = (high - low)[None]

    def scaled(current):
        parts = current.astype(jnp.float32).reshape(vectors, count_v, count_c)
        term = total[...].reshape(vectors, count_v, count_c)
        return ((gap * parts + term - CENTER * parts) / HALF).reshape(flat_rows, count_c)

    kernel_term(start_ref)
    first[...] = scaled(start_ref[...]).astype(jnp.bfloat16)
    kernel_term(first)
    total[...] = 2.0 * scaled(first[...]) - start_ref[...].astype(jnp.float32)

    quads = flat_rows // 4
    part = [total[pl.ds(k, quads, stride=4), :] for k in range(4)]
    third = LANES - count_c
    flat[pl.ds(0, quads, stride=3), :] = jnp.concatenate([part[0], part[1][:, :third]], axis=1)
    flat[pl.ds(1, quads, stride=3), :] = jnp.concatenate([part[1][:, third:], part[2][:, : 2 * third]], axis=1)
    flat[pl.ds(2, quads, stride=3), :] = jnp.concatenate([part[2][:, 2 * third :], part[3]], axis=1)
    out_ref[...] = flat[...].astype(jnp.bfloat16)


def on_device(amplitudes, pairs, stored_k, orbitals, valence_energy, conduction_energy, screened):
    transfers = stored_k.shape[0]
    count_v = valence_energy.shape[1]
    count_c = conduction_energy.shape[1]
    vectors, pair_count, flat_size = amplitudes.shape[1:]
    pair = lax.axis_index("row")
    column = lax.axis_index("col")
    rows_axis, cols = lax.axis_size("row"), lax.axis_size("col")
    devices = rows_axis * cols
    points = orbitals.shape[2] * devices
    share = vectors // cols
    flat_rows = share * count_v
    padded = 16
    smem = pl.BlockSpec(memory_space=pltpu.SMEM)
    vmem = pl.BlockSpec(memory_space=pltpu.VMEM)
    anywhere = pl.BlockSpec(memory_space=pl.ANY)
    limit = pltpu.CompilerParams(vmem_limit_bytes=VMEM_LIMIT)
    width = PARTS * LANES
    swap = [(0, 1), (1, 0)]
    ring = [(r, c) for r in range(rows_axis) for c in range(cols)]
    there = [(r * cols + c, (r + 1 - 2 * c) % rows_axis * cols + c) for r, c in ring]
    back = [(target, source) for source, target in there]

    wishes = pairs[0].T
    message = pl.pallas_call(
        pack_kernel,
        out_shape=jax.ShapeDtypeStruct((transfers, 2, width + LANES), jnp.bfloat16),
        in_specs=[smem, vmem, vmem],
        out_specs=vmem,
        compiler_params=pltpu.CompilerParams(vmem_limit_bytes=2 * VMEM_LIMIT),
    )(wishes, stored_k.reshape(1, transfers), orbitals)
    table = lax.all_to_all(message, "pb", 0, 0, tiled=True)

    start = lax.dynamic_slice(
        amplitudes[0],
        (column * share, pair, 0),
        (share, 1, flat_size),
        allow_negative_indices=False,
    ).reshape(flat_rows, count_c)
    w_own, _ = lax.optimization_barrier((screened[0], message))
    w_there = lax.ppermute(w_own, ("row", "col"), there)
    w_back = lax.ppermute(w_own, ("row", "col"), back)

    table, start = lax.optimization_barrier((table, start))
    w_next, _ = lax.optimization_barrier((w_there, table))
    w_far = lax.ppermute(w_next, ("row", "col"), there)

    wanted = table[:, 0, width : width + 2 * pair_count].astype(jnp.int32)
    chosen = pl.pallas_call(
        select_kernel,
        out_shape=jax.ShapeDtypeStruct((transfers * pair_count, 2, width), jnp.bfloat16),
        in_specs=[smem, vmem],
        out_specs=vmem,
        compiler_params=limit,
    )(wanted, table)
    own = lax.all_to_all(chosen, ("pb", "row"), 0, 0, tiled=True)

    w_core = [w_own, w_there, w_back, w_far]
    w_tiles = w_core + [lax.ppermute(tile, "col", swap) for tile in w_core]
    other = lax.ppermute(own, "col", swap)

    result = pl.pallas_call(
        steps_kernel,
        out_shape=jax.ShapeDtypeStruct((flat_rows * count_c // LANES, LANES), jnp.bfloat16),
        in_specs=[smem, vmem, vmem, vmem, vmem, vmem] + [anywhere] * devices,
        out_specs=vmem,
        scratch_shapes=[
            pltpu.VMEM((count_v, points), jnp.float32),
            pltpu.VMEM((count_c, points), jnp.bfloat16),
            pltpu.VMEM((devices,) + screened.shape[1:], jnp.bfloat16),
            pltpu.VMEM((padded, points), jnp.float32),
            pltpu.VMEM((padded, points), jnp.float32),
            pltpu.VMEM((flat_rows, count_c), jnp.float32),
            pltpu.VMEM((flat_rows, count_c), jnp.bfloat16),
            pltpu.VMEM((flat_rows * count_c // LANES, LANES), jnp.float32),
            pltpu.SemaphoreType.DMA((devices,)),
        ],
        compiler_params=limit,
    )(wishes, valence_energy, conduction_energy, own, other, start, *w_tiles)

    mine = result.reshape(share, flat_size // LANES, LANES)
    across = lax.all_gather(mine, "row")
    theirs = lax.ppermute(across, "col", swap)
    both = jnp.where(column == 0, jnp.stack([across, theirs]), jnp.stack([theirs, across]))
    return both.transpose(0, 2, 1, 3, 4).reshape(1, vectors, pair_count, flat_size)


def solution(mesh):
    return jax.shard_map(
        on_device,
        mesh=mesh,
        in_specs=(
            P("pb", None, None, None),
            P("pb", None, None),
            P(),
            P("pb", None, ("row", "col")),
            P(),
            P(),
            P("pb", "row", "col"),
        ),
        out_specs=P("pb", None, None, None),
        check_vma=False,
    )
```
